32 devices in a mesh: runs: 2 (over y), tag: 8 (over z, x), strip: 2 (over core).
Axes of the slice: x: 2, y: 2, z: 4, core: 2. Of those that a mesh axis runs over, the one named last changes fastest.
Arguments:
- tracer: float32 [32, 128, 2048], P(('runs', 'tag'), 'strip'), parts along dimension 0, may hold values from 0.1 to 3
- water_depth: float32 [256, 2048], P(('runs', 'strip'), 'tag'), parts along dimension 0, may hold values from 1 to 3
- flow_east: float32 [256, 2048], P(('runs', 'strip'), 'tag'), parts along dimension 0, may hold values from -0.5 to 0.5
- flow_south: float32 [256, 2048], P(('runs', 'strip'), 'tag'), parts along dimension 0, may hold values from -0.5 to 0.5
- bed_level: float32 [128, 2048], P('strip', 'tag'), may hold values from 0 to 1
- wet_mask: int32 [256, 2048], P(('runs', 'strip')), parts along dimension 0, may hold values 0 or 1
- land_codes: int32 [128, 2048], P('strip'), may hold values from 0 to 3
- outfall: int32 [16], replicated, may hold values from 0 to 262143
- outfall_loads: float32 [32], P('runs'), parts along dimension 0, may hold values from 2 to 20
Outputs:
- tracer_next: float32 [32, 128, 2048], P(('runs', 'tag'), 'strip'), parts along dimension 0
- depth_next: float32 [256, 2048], P(('runs', 'strip'), 'tag'), parts along dimension 0
- east_next: float32 [256, 2048], P(('runs', 'strip'), 'tag'), parts along dimension 0
- south_next: float32 [256, 2048], P(('runs', 'strip'), 'tag'), parts along dimension 0
The draws below stay inside these ranges and needn't reach their ends.
There are 2 independent parts, one for each index of `runs`. The reference program is written for one: setup_inputs(seed, part) draws one part's arguments, and reference() takes and returns one part's arrays. A program takes and returns all parts, laid end to end along the dimension named above; an argument that names none is the same for every part. Nothing has to cross between parts.
Inputs may be any that keep to these rules, and one draw needn't show every extreme that they name: `wet_mask`: 1 marks a wet cell. `land_codes`: 0 open water, 1 quay wall, 2 beach, 3 river mouth. `outfall`: flat cell index row * 2048 + column inside the window.
All inputs are finite; a program needn't handle non-finite values. No bound on the sum of `wet_mask` on one device may be relied on, other than what follows from the above.
Results may differ from the reference program's by a relative error of at most 0.00012.
Values sent between devices are 32-bit elements; how exact they have to be, the bound alone decides.
A program may use at most 64 MiB of HBM per device.

```python
import math
import jax
import jax.numpy as jnp
from jax import lax

TAGS = 16
COLUMNS = 2048
ROWS = 128
SUBSTEPS = 4


def place_ends(entries, stream_key, least, largest):
    dims = entries.shape
    spot = [jax.random.randint(jax.random.fold_in(stream_key, axis), (), 0, dims[axis]) for axis in range(len(dims))]
    entries = entries.at[tuple(spot)].set(least)
    longest = dims.index(max(dims))
    spot[longest] = (spot[longest] + 1) % dims[longest]
    return entries.at[tuple(spot)].set(largest)


def level_of(rng, extent, pieces, least, largest):
    def one(position, parts):
        steps = jax.random.uniform(jax.random.fold_in(jax.random.fold_in(rng, 6), position), (parts,), jnp.float32, least / len(pieces), largest / len(pieces))
        return jnp.repeat(jnp.exp(steps), extent[position] // parts).reshape((-1,) + (1,) * (len(extent) - position - 1))

    gain = one(*pieces[0])
    for cut in pieces[1:]:
        gain = gain * one(*cut)
    return gain


def setup_inputs(seed: int = 0, part: int = 0) -> dict:
    key_of = jax.random.split(jax.random.key(seed), 10)
    own_keys = jax.random.split(jax.random.fold_in(key_of[9], part), 10)
    tracer = jnp.clip(jnp.exp(math.log(3.0) - 3.4011974 * jax.random.uniform(own_keys[0], (TAGS, ROWS, COLUMNS), jnp.float32) ** level_of(own_keys[0], (TAGS, ROWS, COLUMNS), ((0, 8), (1, 2)), -0.2, 0.2)), 0.1, 3.0)
    water_depth = jnp.clip(1.0 + 2.0 * jax.random.uniform(own_keys[1], (ROWS, COLUMNS), jnp.float32) ** level_of(own_keys[1], (ROWS, COLUMNS), ((0, 2), (1, 8)), -0.2, 0.2), 1.0, 3.0)
    flow_east = jnp.clip(jax.random.uniform(own_keys[2], (ROWS, COLUMNS), jnp.float32, -0.5, 0.5) * level_of(own_keys[2], (ROWS, COLUMNS), ((0, 2), (1, 8)), -0.4, 0.0), -0.5, 0.5)
    flow_south = jnp.clip(jax.random.uniform(own_keys[3], (ROWS, COLUMNS), jnp.float32, -0.5, 0.5) * level_of(own_keys[3], (ROWS, COLUMNS), ((0, 2), (1, 8)), -0.4, 0.0), -0.5, 0.5)
    bed_level = jnp.clip(1.0 * jax.random.uniform(key_of[4], (ROWS, COLUMNS), jnp.float32) ** level_of(key_of[4], (ROWS, COLUMNS), ((0, 2), (1, 8)), -0.2, 0.2), 0.0, 1.0)
    wet_mask = place_ends((jax.random.randint(own_keys[5], (ROWS, COLUMNS), 0, 8) < 7).astype(jnp.int32), jax.random.fold_in(own_keys[5], 1), 0, 1)
    land_codes = place_ends(jax.random.randint(key_of[6], (ROWS, COLUMNS), 0, 4), jax.random.fold_in(key_of[6], 1), 0, 3).astype(jnp.int32)
    outfall = place_ends(jax.random.randint(key_of[7], (TAGS,), 0, ROWS * COLUMNS), jax.random.fold_in(key_of[7], 1), 0, (ROWS * COLUMNS) - 1).astype(jnp.int32)
    outfall_loads = jnp.clip(jnp.exp(jax.random.uniform(own_keys[8], (TAGS,), jnp.float32, math.log(2.0), math.log(20.0))), 2.0, 20.0)
    return {"tracer": tracer, "water_depth": water_depth, "flow_east": flow_east, "flow_south": flow_south, "bed_level": bed_level, "wet_mask": wet_mask, "land_codes": land_codes, "outfall": outfall, "outfall_loads": outfall_loads}


STEP_RATIO = 0.2
GRAVITY_STEP = 0.1
COURANT = 0.2
DECAY_RATE = 0.005
SOURCE_STEP = 0.25
FRICTION_TABLE = (0.0, 0.3, 1.0, 2.5)
DISPERSION_TABLE = (0.02, 0.05, 0.08, 0.1)


def lookup(land_codes, lookup_table):
    result = jnp.zeros(land_codes.shape, jnp.float32)
    for code_value in range(4):
        result = result + jnp.where(land_codes == code_value, lookup_table[code_value], 0.0)
    return result


def shallow_step(padded, land_codes):
    water_depth = padded[0, 1:-1, 1:-1]
    surface = padded[0] + padded[3]
    flow_east = padded[1]
    flow_south = padded[2]
    divergence = 0.5 * (flow_east[1:-1, 2:] - flow_east[1:-1, :-2]) + 0.5 * (flow_south[2:, 1:-1] - flow_south[:-2, 1:-1])
    depth_next = water_depth - STEP_RATIO * divergence
    friction = 1.0 + lookup(land_codes, FRICTION_TABLE)
    slope_east = 0.5 * (surface[1:-1, 2:] - surface[1:-1, :-2])
    slope_south = 0.5 * (surface[2:, 1:-1] - surface[:-2, 1:-1])
    east_next = (flow_east[1:-1, 1:-1] - GRAVITY_STEP * water_depth * slope_east) / friction
    south_next = (flow_south[1:-1, 1:-1] - GRAVITY_STEP * water_depth * slope_south) / friction
    return depth_next, east_next, south_next


def releases(outfall, outfall_loads, row_start, col_start, rows_here, cols_here):
    row_ids = outfall // COLUMNS - row_start
    col_ids = outfall % COLUMNS - col_start
    row_hit = lax.broadcasted_iota(jnp.int32, (1, rows_here, 1), 1) == row_ids[:, None, None]
    col_hit = lax.broadcasted_iota(jnp.int32, (1, 1, cols_here), 2) == col_ids[:, None, None]
    return jnp.where(row_hit & col_hit, SOURCE_STEP * outfall_loads[:, None, None], 0.0)


def advance(padded, tracer, speed_east, speed_south, dispersion, wet_cells, source, total_tracer):
    west_side = padded[:, 1:-1, :-2]
    east_side = padded[:, 1:-1, 2:]
    north_side = padded[:, :-2, 1:-1]
    south_side = padded[:, 2:, 1:-1]
    east_going = jnp.maximum(speed_east, 0.0)
    west_going = jnp.minimum(speed_east, 0.0)
    south_going = jnp.maximum(speed_south, 0.0)
    north_going = jnp.minimum(speed_south, 0.0)
    advected = (tracer
                - COURANT * (east_going * (tracer - west_side) + west_going * (east_side - tracer))
                - COURANT * (south_going * (tracer - north_side) + north_going * (south_side - tracer))
                + dispersion * (west_side + east_side + north_side + south_side - 4.0 * tracer))
    return wet_cells * (advected + source) / (1.0 + DECAY_RATE * total_tracer)


def reference(tracer, water_depth, flow_east, flow_south, bed_level, wet_mask, land_codes, outfall, outfall_loads):
    stacked = jnp.stack([water_depth, flow_east, flow_south, bed_level])
    padded = jnp.pad(stacked, ((0, 0), (1, 1), (1, 1)))
    depth_next, east_next, south_next = shallow_step(padded, land_codes)
    wet_cells = wet_mask.astype(jnp.float32)
    speed_east = wet_cells * east_next / depth_next
    speed_south = wet_cells * south_next / depth_next
    dispersion = lookup(land_codes, DISPERSION_TABLE)
    source = releases(outfall, outfall_loads, 0, 0, tracer.shape[1], tracer.shape[2])
    for substep in range(SUBSTEPS):
        total_tracer = jnp.sum(tracer, axis=0)
        padded_tracer = jnp.pad(tracer, ((0, 0), (1, 1), (1, 1)))
        tracer = advance(padded_tracer, tracer, speed_east, speed_south, dispersion, wet_cells, source, total_tracer)
    return (tracer, depth_next, east_next, south_next)
```

```python
import functools
import jax
import jax.numpy as jnp
from jax import lax
from jax.experimental import pallas as pl
from jax.experimental.pallas import tpu as pltpu
from jax.sharding import PartitionSpec as P

COLUMNS = 2048
SUBSTEPS = 4
MESH = pl.DeviceIdType.MESH


STEP_RATIO = 0.2
GRAVITY_STEP = 0.1
COURANT = 0.2
DECAY_RATE = 0.005
SOURCE_STEP = 0.25
FRICTION_TABLE = (0.0, 0.3, 1.0, 2.5)
DISPERSION_TABLE = (0.02, 0.05, 0.08, 0.1)


def extended(cells, sides, width):
    for axis, dim in sides:
        count = lax.axis_size(axis)
        ends = count - 1
        head = lax.slice_in_dim(cells, 0, width, axis=dim)
        tail = lax.slice_in_dim(cells, cells.shape[dim] - width, cells.shape[dim], axis=dim)
        cells = jnp.concatenate(
            [
                lax.ppermute(tail, axis, [(i, (i + 1) % count) for i in range(ends)]),
                cells,
                lax.ppermute(head, axis, [((i + 1) % count, i) for i in range(ends)]),
            ],
            axis=dim,
        )
    return cells


def lookup(land_codes, lookup_table):
    result = jnp.zeros(land_codes.shape, jnp.float32)
    for code_value in range(4):
        result = result + jnp.where(land_codes == code_value, lookup_table[code_value], 0.0)
    return result


def shallow_step(padded, land_codes):
    water_depth = padded[0, 1:-1, 1:-1]
    surface = padded[0] + padded[3]
    flow_east = padded[1]
    flow_south = padded[2]
    divergence = 0.5 * (flow_east[1:-1, 2:] - flow_east[1:-1, :-2]) + 0.5 * (
        flow_south[2:, 1:-1] - flow_south[:-2, 1:-1]
    )
    depth_next = water_depth - STEP_RATIO * divergence
    friction = 1.0 + lookup(land_codes, FRICTION_TABLE)
    slope_east = 0.5 * (surface[1:-1, 2:] - surface[1:-1, :-2])
    slope_south = 0.5 * (surface[2:, 1:-1] - surface[:-2, 1:-1])
    east_next = (flow_east[1:-1, 1:-1] - GRAVITY_STEP * water_depth * slope_east) / friction
    south_next = (flow_south[1:-1, 1:-1] - GRAVITY_STEP * water_depth * slope_south) / friction
    return (depth_next, east_next, south_next)


def releases(outfall, outfall_loads, row_start, col_start, rows_here, cols_here):
    row_ids = outfall // COLUMNS - row_start
    col_ids = outfall % COLUMNS - col_start
    row_hit = lax.broadcasted_iota(jnp.int32, (1, rows_here, 1), 1) == row_ids[:, None, None]
    col_hit = lax.broadcasted_iota(jnp.int32, (1, 1, cols_here), 2) == col_ids[:, None, None]
    return jnp.where(row_hit & col_hit, SOURCE_STEP * outfall_loads[:, None, None], 0.0)


def summed_releases(outfall, outfall_loads, row_start, rows_here, cols_here):
    row_ids = outfall // COLUMNS - row_start
    col_ids = outfall % COLUMNS
    row_table = (lax.broadcasted_iota(jnp.int32, (rows_here, 1), 0) == row_ids[None, :]).astype(
        jnp.float32
    )
    col_table = jnp.where(
        lax.broadcasted_iota(jnp.int32, (1, cols_here), 1) == col_ids[:, None],
        SOURCE_STEP * outfall_loads[:, None],
        0.0,
    )
    return jnp.dot(
        row_table, col_table, precision=lax.Precision.HIGHEST, preferred_element_type=jnp.float32
    )


def advance(padded, tracer, speed_east, speed_south, dispersion, wet_cells, source, total_tracer):
    west_side = padded[:, 1:-1, :-2]
    east_side = padded[:, 1:-1, 2:]
    north_side = padded[:, :-2, 1:-1]
    south_side = padded[:, 2:, 1:-1]
    east_going = jnp.maximum(speed_east, 0.0)
    west_going = jnp.minimum(speed_east, 0.0)
    south_going = jnp.maximum(speed_south, 0.0)
    north_going = jnp.minimum(speed_south, 0.0)
    advected = (
        tracer
        - COURANT * (east_going * (tracer - west_side) + west_going * (east_side - tracer))
        - COURANT * (south_going * (tracer - north_side) + north_going * (south_side - tracer))
        + dispersion * (west_side + east_side + north_side + south_side - 4.0 * tracer)
    )
    return wet_cells * (advected + source) / (1.0 + DECAY_RATE * total_tracer)


def padded_rows(tracer):
    padded_tracer = extended(tracer, (("strip", 1),), 1)
    return jnp.pad(padded_tracer, ((0, 0), (0, 0), (1, 1)))


def shards(
    tracer,
    water_depth,
    flow_east,
    flow_south,
    bed_level,
    wet_mask,
    land_codes,
    outfall,
    outfall_loads,
):
    rows_here = water_depth.shape[0]
    tile_cols = water_depth.shape[1]
    tags_here = tracer.shape[0]
    tag_place = lax.axis_index("tag")
    strip_place = lax.axis_index("strip")
    col_start = tag_place * tile_cols
    row_start = strip_place * rows_here
    codes_tile = lax.dynamic_slice_in_dim(land_codes, col_start, tile_cols, 1)
    wet_tile = lax.dynamic_slice_in_dim(wet_mask, col_start, tile_cols, 1).astype(jnp.float32)
    stacked = jnp.stack([water_depth, flow_east, flow_south, bed_level])
    padded = extended(stacked, (("tag", 2), ("strip", 1)), 1)
    depth_next, east_next, south_next = shallow_step(padded, codes_tile)
    speeds = jnp.stack([wet_tile * east_next / depth_next, wet_tile * south_next / depth_next])
    gathered = lax.all_gather(speeds, "tag", axis=2, tiled=True)
    wet_cells = wet_mask.astype(jnp.float32)
    dispersion = lookup(land_codes, DISPERSION_TABLE)
    own_outfall = lax.dynamic_slice_in_dim(outfall, tag_place * tags_here, tags_here)
    own_loads = lax.dynamic_slice_in_dim(outfall_loads, tag_place * tags_here, tags_here)
    source = releases(own_outfall, own_loads, row_start, 0, rows_here, tracer.shape[2])
    total_now = lax.psum(jnp.sum(tracer, axis=0), "tag")
    source_total = summed_releases(outfall, outfall_loads, row_start, rows_here, tracer.shape[2])[
        None
    ]
    for substep in range(SUBSTEPS):
        padded_tracer = padded_rows(tracer)
        tracer = advance(
            padded_tracer,
            tracer,
            gathered[0],
            gathered[1],
            dispersion,
            wet_cells,
            source,
            total_now,
        )
        if substep + 1 < SUBSTEPS:
            padded_total = extended(total_now[None], (("strip", 1),), 1)
            padded_total = jnp.pad(padded_total, ((0, 0), (0, 0), (1, 1)))
            total_now = advance(
                padded_total,
                total_now[None],
                gathered[0],
                gathered[1],
                dispersion,
                wet_cells,
                source_total,
                total_now,
            )[0]
    return (tracer, depth_next, east_next, south_next)


def pick(codes, table):
    return jnp.where(
        codes == 0,
        table[0],
        jnp.where(codes == 1, table[1], jnp.where(codes == 2, table[2], table[3])),
    )


def flood_kernel(
    n_tag,
    tracer_ref,
    depth_ref,
    east_ref,
    south_ref,
    bed_ref,
    wet_ref,
    code_ref,
    outfall_ref,
    loads_ref,
    tracer_out,
    depth_out,
    east_out,
    south_out,
    cols_out,
    cols_in,
    rows_out,
    rows_in,
    part,
    from_x,
    red,
    from_z,
    speeds,
    totals,
    coef,
    wet_cells,
    release,
    field,
    edge_out,
    edge_in,
    halo_send,
    halo_recv,
    x_send,
    x_recv,
    z_send,
    z_recv,
    speed_send,
    speed_recv,
    total_send,
    total_recv,
    edge_send,
    edge_recv,
):
    tags, rows, cols = tracer_ref.shape
    tile = depth_ref.shape[1]
    n_z = n_tag // 2
    place = lax.axis_index("tag")
    strip = lax.axis_index("strip")
    z, x = place // 2, place % 2
    other_x, other_strip = 1 - x, 1 - strip
    partner = z * 2 + other_x
    blocks = rows // 8

    def peer(k):
        result, bit = z, 1
        while bit < n_z:
            if k & bit:
                result = result + bit - 2 * bit * ((result // bit) % 2)
            bit *= 2
        return result

    def to(axis, index, src, dst, send, recv):
        return pltpu.make_async_remote_copy(
            src_ref=src,
            dst_ref=dst,
            send_sem=send,
            recv_sem=recv,
            device_id={axis: index},
            device_id_type=MESH,
        )

    def span(slot):
        return pl.ds(pl.multiple_of(slot * tile, tile), tile)

    sent = []

    def go(copy):
        copy.start()
        sent.append(copy)

    barrier = pltpu.get_barrier_semaphore()
    cols_in[...] = jnp.zeros_like(cols_in)
    for k in range(1, n_tag):
        pl.semaphore_signal(
            barrier, inc=1, device_id={"tag": lax.rem(place + k, n_tag)}, device_id_type=MESH
        )
    pl.semaphore_signal(barrier, inc=1, device_id={"strip": other_strip}, device_id_type=MESH)

    water = depth_ref[...]
    east = east_ref[...]
    south = south_ref[...]
    surface = water + bed_ref[...]
    first = lax.broadcasted_iota(jnp.int32, (rows, 128), 1) == 0
    cols_out[0] = jnp.where(first, east[:, 0:1], surface[:, 0:1])
    cols_out[1] = jnp.where(first, east[:, tile - 1 : tile], surface[:, tile - 1 : tile])
    upper = strip == 0
    edge_first = lax.broadcasted_iota(jnp.int32, (8, tile), 0) == 0
    rows_out[...] = jnp.where(
        edge_first,
        jnp.where(upper, south[rows - 1 : rows], south[0:1]),
        jnp.where(upper, surface[rows - 1 : rows], surface[0:1]),
    )
    edge_out[...] = jnp.zeros_like(edge_out)
    for f in range(tags):
        edge_out[0, f : f + 1, :] = jnp.where(
            upper, tracer_ref[f, rows - 1 : rows, :], tracer_ref[f, 0:1, :]
        )
    for slot in range(n_tag):
        share = tracer_ref[0, :, slot * tile : (slot + 1) * tile]
        for f in range(1, tags):
            share = share + tracer_ref[f, :, slot * tile : (slot + 1) * tile]
        part[slot % 2, slot // 2] = share

    pl.semaphore_wait(barrier, n_tag)

    to_west = to("tag", place - 1, cols_out.at[0], cols_in.at[1], halo_send.at[0], halo_recv.at[1])
    to_east = to("tag", place + 1, cols_out.at[1], cols_in.at[0], halo_send.at[1], halo_recv.at[0])
    to_strip = to("strip", other_strip, rows_out, rows_in, halo_send.at[2], halo_recv.at[2])

    @pl.when(place > 0)
    def _():
        to_west.start()

    @pl.when(place < n_tag - 1)
    def _():
        to_east.start()

    go(to_strip)
    for k in reversed(range(n_z)):
        go(
            to(
                "tag",
                partner,
                part.at[other_x, peer(k)],
                from_x.at[k],
                x_send.at[k],
                x_recv.at[k],
            )
        )
    go(to("strip", other_strip, edge_out.at[0], edge_in.at[0], edge_send.at[0], edge_recv.at[0]))

    @pl.when(place > 0)
    def _():
        to_east.wait_recv()

    @pl.when(place < n_tag - 1)
    def _():
        to_west.wait_recv()

    to_strip.wait_recv()
    lane = lax.broadcasted_iota(jnp.int32, (rows, tile), 1)
    row = lax.broadcasted_iota(jnp.int32, (rows, tile), 0)

    def west_of(cells, edge):
        return jnp.where(lane == 0, edge, pltpu.roll(cells, 1, 1))

    def east_of(cells, edge):
        return jnp.where(lane == tile - 1, edge, pltpu.roll(cells, tile - 1, 1))

    def north_of(cells, edge):
        return jnp.where(row == 0, jnp.where(upper, 0.0, edge), pltpu.roll(cells, 1, 0))

    def south_of(cells, edge):
        return jnp.where(row == rows - 1, jnp.where(upper, edge, 0.0), pltpu.roll(cells, rows - 1, 0))

    west_in, east_in, strip_in = cols_in[0], cols_in[1], rows_in[...]
    divergence = 0.5 * (
        east_of(east, east_in[:, 0:1]) - west_of(east, west_in[:, 0:1])
    ) + 0.5 * (south_of(south, strip_in[0:1]) - north_of(south, strip_in[0:1]))
    depth_next = water - STEP_RATIO * divergence
    own_codes = code_ref[:, span(place)]
    own_wet = wet_ref[:, span(place)].astype(jnp.float32)
    friction = 1.0 + pick(own_codes, FRICTION_TABLE)
    slope_east = 0.5 * (east_of(surface, east_in[:, 1:2]) - west_of(surface, west_in[:, 1:2]))
    slope_south = 0.5 * (south_of(surface, strip_in[1:2]) - north_of(surface, strip_in[1:2]))
    east_next = (east - GRAVITY_STEP * water * slope_east) / friction
    south_next = (south - GRAVITY_STEP * water * slope_south) / friction
    depth_out[...] = depth_next
    east_out[...] = east_next
    south_out[...] = south_next
    speeds[place, 0] = own_wet * east_next / depth_next
    speeds[place, 1] = own_wet * south_next / depth_next

    def gather(held, send, recv):
        for k in range(1, n_z):
            go(to("tag", peer(k) * 2 + x, held.at[place], held.at[place], send.at[k], recv.at[place]))
        go(to("tag", partner, held.at[place], held.at[place], send.at[0], recv.at[place]))

    def arrived(held, send, recv, slot):
        to("tag", partner, held.at[slot], held.at[slot], send.at[0], recv.at[slot]).wait_recv()

    def pass_on(held, send, recv, k):
        slot = peer(k) * 2 + x
        arrived(held, send, recv, slot)
        go(to("tag", partner, held.at[slot], held.at[slot], send.at[n_z - 1 + k], recv.at[slot]))

    gather(speeds, speed_send, speed_recv)

    for k in reversed(range(n_z)):
        into = from_x.at[k]
        to("tag", partner, into, into, x_send.at[k], x_recv.at[k]).wait_recv()
        red[k] = part[x, peer(k)] + into[...]
        if k:
            go(to("tag", peer(k) * 2 + x, red.at[k], from_z.at[k], z_send.at[k], z_recv.at[k]))

    def prepare(i, carry):
        at = pl.multiple_of(i * 8, 8)
        ids = (
            (strip * rows + at + lax.broadcasted_iota(jnp.int32, (8, cols), 0)) * COLUMNS
            + lax.broadcasted_iota(jnp.int32, (8, cols), 1)
        )
        for f in range(tags):
            t = place * tags + f
            release[f, pl.ds(at, 8), :] = jnp.where(
                ids == outfall_ref[t], SOURCE_STEP * loads_ref[t], 0.0
            )
            field[0, f, pl.ds(at + 8, 8), :] = tracer_ref[f, pl.ds(at, 8), :]
        all_tags = jnp.zeros((8, cols), jnp.float32)
        for t in range(outfall_ref.shape[0]):
            all_tags = all_tags + jnp.where(ids == outfall_ref[t], SOURCE_STEP * loads_ref[t], 0.0)
        release[tags, pl.ds(at, 8), :] = all_tags
        wet_cells[pl.ds(at, 8), :] = wet_ref[pl.ds(at, 8), :].astype(jnp.float32)
        return carry

    lax.fori_loop(0, blocks, prepare, 0)

    own_total = red[0]
    for k in range(1, n_z):
        to("tag", partner, red.at[k], from_z.at[k], z_send.at[k], z_recv.at[k]).wait_recv()
        own_total = own_total + from_z[k]
    totals[place] = own_total
    gather(totals, total_send, total_recv)

    def weigh(slot):
        go_east = speeds[slot, 0]
        go_south = speeds[slot, 1]
        spread = pick(code_ref[:, span(slot)], DISPERSION_TABLE)
        west = spread + COURANT * jnp.maximum(go_east, 0.0)
        east = spread - COURANT * jnp.minimum(go_east, 0.0)
        north = spread + COURANT * jnp.maximum(go_south, 0.0)
        south = spread - COURANT * jnp.minimum(go_south, 0.0)
        coef[0, :, span(slot)] = 1.0 - ((west + east) + (north + south))
        column = slot * tile + lane
        coef[1, :, span(slot)] = jnp.where(column == 0, 0.0, west)
        coef[2, :, span(slot)] = jnp.where(column == cols - 1, 0.0, east)
        coef[3, :, span(slot)] = jnp.where((row == 0) & upper, 0.0, north)
        coef[4, :, span(slot)] = jnp.where((row == rows - 1) & (strip == 1), 0.0, south)

    def settle(slot):
        field[0, tags, 8 : 8 + rows, span(slot)] = totals[slot]

    weigh(place)
    for k in range(1, n_z):
        pass_on(speeds, speed_send, speed_recv, k)
        weigh(peer(k) * 2 + x)
    for k in range(n_z):
        slot = peer(k) * 2 + other_x
        arrived(speeds, speed_send, speed_recv, slot)
        weigh(slot)
        if k + 1 < n_z:
            pass_on(totals, total_send, total_recv, k + 1)
            settle(peer(k + 1) * 2 + x)
    settle(place)
    for k in range(n_z):
        slot = peer(k) * 2 + other_x
        arrived(totals, total_send, total_recv, slot)
        settle(slot)

    last = jnp.where(upper, blocks - 1, 0)

    def edge_row(now, f):
        return jnp.where(
            upper, field[now, f, 7 + rows : 8 + rows, :], field[now, f, 8:9, :]
        )

    def exchange(n):
        return to(
            "strip", other_strip, edge_out.at[n], edge_in.at[n], edge_send.at[n], edge_recv.at[n]
        )

    edge_out[1, tags : tags + 1, :] = edge_row(0, tags)
    go(exchange(1))

    def put_halo(n, now, fields):
        for f in fields:
            got = edge_in[n, f : f + 1, :]
            field[now, f, 7:8, :] = got
            field[now, f, 8 + rows : 9 + rows, :] = got

    exchange(0).wait_recv()
    put_halo(0, 0, range(tags))
    exchange(1).wait_recv()
    put_halo(1, 0, [tags])

    for substep in range(SUBSTEPS):
        now, later = substep % 2, 1 - substep % 2
        ends = substep == SUBSTEPS - 1
        if substep:
            exchange(substep + 1).wait_recv()
            put_halo(substep + 1, now, range(tags + 1))

        def block(i, carry):
            at = pl.multiple_of(lax.rem(last + i, blocks) * 8, 8)
            here = pl.ds(at, 8)
            rate = wet_cells[here, :] / (1.0 + DECAY_RATE * field[now, tags, pl.ds(at + 8, 8), :])
            for f in range(tags if ends else tags + 1):
                wide = field[now, f, pl.ds(at, 24), :]
                cell = wide[8:16]
                value = (
                    coef[0, here, :] * cell
                    + coef[1, here, :] * pltpu.roll(cell, 1, 1)
                    + coef[2, here, :] * pltpu.roll(cell, cols - 1, 1)
                    + coef[3, here, :] * wide[7:15]
                    + coef[4, here, :] * wide[9:17]
                    + release[f, here, :]
                ) * rate
                if ends:
                    tracer_out[f, here, :] = value
                else:
                    field[later, f, pl.ds(at + 8, 8), :] = value
            if not ends:

                @pl.when(i == 0)
                def _():
                    for f in range(tags + 1):
                        edge_out[substep + 2, f : f + 1, :] = edge_row(later, f)
                    exchange(substep + 2).start()

            return carry

        lax.fori_loop(0, blocks, block, 0)

    for n in range(SUBSTEPS - 1):
        exchange(n + 2).wait_send()
    for copy in sent:
        copy.wait_send()

    @pl.when(place > 0)
    def _():
        to_west.wait_send()

    @pl.when(place < n_tag - 1)
    def _():
        to_east.wait_send()


def fused(n_tag, *arrays):
    tracer, water = arrays[0], arrays[1]
    tags, rows, cols = tracer.shape
    tile = water.shape[1]
    n_z = n_tag // 2
    f32 = jnp.float32
    dma = pltpu.SemaphoreType.DMA
    vmem = pl.BlockSpec(memory_space=pltpu.VMEM)
    smem = pl.BlockSpec(memory_space=pltpu.SMEM)
    plane = jax.ShapeDtypeStruct(water.shape, f32)
    return pl.pallas_call(
        functools.partial(flood_kernel, n_tag),
        out_shape=(jax.ShapeDtypeStruct(tracer.shape, f32), plane, plane, plane),
        in_specs=[vmem] * 7 + [smem] * 2,
        out_specs=(vmem,) * 4,
        scratch_shapes=[
            pltpu.VMEM((2, rows, 128), f32),
            pltpu.VMEM((2, rows, 128), f32),
            pltpu.VMEM((8, tile), f32),
            pltpu.VMEM((8, tile), f32),
            pltpu.VMEM((2, n_z, rows, tile), f32),
            pltpu.VMEM((n_z, rows, tile), f32),
            pltpu.VMEM((n_z, rows, tile), f32),
            pltpu.VMEM((n_z, rows, tile), f32),
            pltpu.VMEM((n_tag, 2, rows, tile), f32),
            pltpu.VMEM((n_tag, rows, tile), f32),
            pltpu.VMEM((5, rows, cols), f32),
            pltpu.VMEM((rows, cols), f32),
            pltpu.VMEM((tags + 1, rows, cols), f32),
            pltpu.VMEM((2, tags + 1, rows + 16, cols), f32),
            pltpu.VMEM((SUBSTEPS + 1, 8, cols), f32),
            pltpu.VMEM((SUBSTEPS + 1, 8, cols), f32),
            dma((3,)),
            dma((3,)),
            dma((n_z,)),
            dma((n_z,)),
            dma((n_z,)),
            dma((n_z,)),
            dma((2 * n_z - 1,)),
            dma((n_tag,)),
            dma((2 * n_z - 1,)),
            dma((n_tag,)),
            dma((SUBSTEPS + 1,)),
            dma((SUBSTEPS + 1,)),
        ],
        compiler_params=pltpu.CompilerParams(
            collective_id=0, has_side_effects=True, vmem_limit_bytes=48 * 1024 * 1024
        ),
    )(*arrays)


def fits(n_tag, n_strip, tags, rows, cols):
    tile = cols // n_tag
    z_power = n_tag % 2 == 0 and (n_tag // 2) & (n_tag // 2 - 1) == 0
    return (
        n_strip == 2 and z_power and n_tag <= 16 and tile % 128 == 0 and rows % 8 == 0 and tags < 8
    )


def solution(mesh):
    in_specs = (
        P(("runs", "tag"), "strip", None),
        P(("runs", "strip"), "tag"),
        P(("runs", "strip"), "tag"),
        P(("runs", "strip"), "tag"),
        P("strip", "tag"),
        P(("runs", "strip"), None),
        P("strip", None),
        P(),
        P("runs"),
    )
    out_specs = (
        P(("runs", "tag"), "strip", None),
        P(("runs", "strip"), "tag"),
        P(("runs", "strip"), "tag"),
        P(("runs", "strip"), "tag"),
    )

    def local(*arrays):
        n_tag, n_strip = mesh.shape["tag"], mesh.shape["strip"]
        if fits(n_tag, n_strip, *arrays[0].shape):
            return fused(n_tag, *arrays)
        return shards(*arrays)

    return jax.shard_map(local, mesh=mesh, in_specs=in_specs, out_specs=out_specs, check_vma=False)
```

```python
import functools
import jax
import jax.numpy as jnp
from jax import lax
from jax.experimental import pallas as pl
from jax.experimental.pallas import tpu as pltpu
from jax.sharding import PartitionSpec as P

COLUMNS = 2048
SUBSTEPS = 4
MESH = pl.DeviceIdType.MESH


STEP_RATIO = 0.2
GRAVITY_STEP = 0.1
COURANT = 0.2
DECAY_RATE = 0.005
SOURCE_STEP = 0.25
FRICTION_TABLE = (0.0, 0.3, 1.0, 2.5)
DISPERSION_TABLE = (0.02, 0.05, 0.08, 0.1)


def extended(cells, sides, width):
    for axis, dim in sides:
        count = lax.axis_size(axis)
        ends = count - 1
        head = lax.slice_in_dim(cells, 0, width, axis=dim)
        tail = lax.slice_in_dim(cells, cells.shape[dim] - width, cells.shape[dim], axis=dim)
        cells = jnp.concatenate(
            [
                lax.ppermute(tail, axis, [(i, (i + 1) % count) for i in range(ends)]),
                cells,
                lax.ppermute(head, axis, [((i + 1) % count, i) for i in range(ends)]),
            ],
            axis=dim,
        )
    return cells


def lookup(land_codes, lookup_table):
    result = jnp.zeros(land_codes.shape, jnp.float32)
    for code_value in range(4):
        result = result + jnp.where(land_codes == code_value, lookup_table[code_value], 0.0)
    return result


def shallow_step(padded, land_codes):
    water_depth = padded[0, 1:-1, 1:-1]
    surface = padded[0] + padded[3]
    flow_east = padded[1]
    flow_south = padded[2]
    divergence = 0.5 * (flow_east[1:-1, 2:] - flow_east[1:-1, :-2]) + 0.5 * (
        flow_south[2:, 1:-1] - flow_south[:-2, 1:-1]
    )
    depth_next = water_depth - STEP_RATIO * divergence
    friction = 1.0 + lookup(land_codes, FRICTION_TABLE)
    slope_east = 0.5 * (surface[1:-1, 2:] - surface[1:-1, :-2])
    slope_south = 0.5 * (surface[2:, 1:-1] - surface[:-2, 1:-1])
    east_next = (flow_east[1:-1, 1:-1] - GRAVITY_STEP * water_depth * slope_east) / friction
    south_next = (flow_south[1:-1, 1:-1] - GRAVITY_STEP * water_depth * slope_south) / friction
    return (depth_next, east_next, south_next)


def releases(outfall, outfall_loads, row_start, col_start, rows_here, cols_here):
    row_ids = outfall // COLUMNS - row_start
    col_ids = outfall % COLUMNS - col_start
    row_hit = lax.broadcasted_iota(jnp.int32, (1, rows_here, 1), 1) == row_ids[:, None, None]
    col_hit = lax.broadcasted_iota(jnp.int32, (1, 1, cols_here), 2) == col_ids[:, None, None]
    return jnp.where(row_hit & col_hit, SOURCE_STEP * outfall_loads[:, None, None], 0.0)


def summed_releases(outfall, outfall_loads, row_start, rows_here, cols_here):
    row_ids = outfall // COLUMNS - row_start
    col_ids = outfall % COLUMNS
    row_table = (lax.broadcasted_iota(jnp.int32, (rows_here, 1), 0) == row_ids[None, :]).astype(
        jnp.float32
    )
    col_table = jnp.where(
        lax.broadcasted_iota(jnp.int32, (1, cols_here), 1) == col_ids[:, None],
        SOURCE_STEP * outfall_loads[:, None],
        0.0,
    )
    return jnp.dot(
        row_table, col_table, precision=lax.Precision.HIGHEST, preferred_element_type=jnp.float32
    )


def advance(padded, tracer, speed_east, speed_south, dispersion, wet_cells, source, total_tracer):
    west_side = padded[:, 1:-1, :-2]
    east_side = padded[:, 1:-1, 2:]
    north_side = padded[:, :-2, 1:-1]
    south_side = padded[:, 2:, 1:-1]
    east_going = jnp.maximum(speed_east, 0.0)
    west_going = jnp.minimum(speed_east, 0.0)
    south_going = jnp.maximum(speed_south, 0.0)
    north_going = jnp.minimum(speed_south, 0.0)
    advected = (
        tracer
        - COURANT * (east_going * (tracer - west_side) + west_going * (east_side - tracer))
        - COURANT * (south_going * (tracer - north_side) + north_going * (south_side - tracer))
        + dispersion * (west_side + east_side + north_side + south_side - 4.0 * tracer)
    )
    return wet_cells * (advected + source) / (1.0 + DECAY_RATE * total_tracer)


def padded_rows(tracer):
    padded_tracer = extended(tracer, (("strip", 1),), 1)
    return jnp.pad(padded_tracer, ((0, 0), (0, 0), (1, 1)))


def shards(
    tracer,
    water_depth,
    flow_east,
    flow_south,
    bed_level,
    wet_mask,
    land_codes,
    outfall,
    outfall_loads,
):
    rows_here = water_depth.shape[0]
    tile_cols = water_depth.shape[1]
    tags_here = tracer.shape[0]
    tag_place = lax.axis_index("tag")
    strip_place = lax.axis_index("strip")
    col_start = tag_place * tile_cols
    row_start = strip_place * rows_here
    codes_tile = lax.dynamic_slice_in_dim(land_codes, col_start, tile_cols, 1)
    wet_tile = lax.dynamic_slice_in_dim(wet_mask, col_start, tile_cols, 1).astype(jnp.float32)
    stacked = jnp.stack([water_depth, flow_east, flow_south, bed_level])
    padded = extended(stacked, (("tag", 2), ("strip", 1)), 1)
    depth_next, east_next, south_next = shallow_step(padded, codes_tile)
    speeds = jnp.stack([wet_tile * east_next / depth_next, wet_tile * south_next / depth_next])
    gathered = lax.all_gather(speeds, "tag", axis=2, tiled=True)
    wet_cells = wet_mask.astype(jnp.float32)
    dispersion = lookup(land_codes, DISPERSION_TABLE)
    own_outfall = lax.dynamic_slice_in_dim(outfall, tag_place * tags_here, tags_here)
    own_loads = lax.dynamic_slice_in_dim(outfall_loads, tag_place * tags_here, tags_here)
    source = releases(own_outfall, own_loads, row_start, 0, rows_here, tracer.shape[2])
    total_now = lax.psum(jnp.sum(tracer, axis=0), "tag")
    source_total = summed_releases(outfall, outfall_loads, row_start, rows_here, tracer.shape[2])[
        None
    ]
    for substep in range(SUBSTEPS):
        padded_tracer = padded_rows(tracer)
        tracer = advance(
            padded_tracer,
            tracer,
            gathered[0],
            gathered[1],
            dispersion,
            wet_cells,
            source,
            total_now,
        )
        if substep + 1 < SUBSTEPS:
            padded_total = extended(total_now[None], (("strip", 1),), 1)
            padded_total = jnp.pad(padded_total, ((0, 0), (0, 0), (1, 1)))
            total_now = advance(
                padded_total,
                total_now[None],
                gathered[0],
                gathered[1],
                dispersion,
                wet_cells,
                source_total,
                total_now,
            )[0]
    return (tracer, depth_next, east_next, south_next)


def pick(codes, table):
    return jnp.where(
        codes == 0,
        table[0],
        jnp.where(codes == 1, table[1], jnp.where(codes == 2, table[2], table[3])),
    )


def flood_kernel(
    n_tag,
    tracer_hbm,
    depth_hbm,
    east_hbm,
    south_hbm,
    bed_hbm,
    wet_hbm,
    code_hbm,
    outfall_hbm,
    loads_hbm,
    tracer_out,
    depth_out,
    east_out,
    south_out,
    tracer_ref,
    depth_ref,
    east_ref,
    south_ref,
    bed_ref,
    wet_ref,
    code_ref,
    outfall_ref,
    loads_ref,
    load_sem,
    cols_out,
    cols_in,
    rows_out,
    rows_in,
    part,
    from_x,
    red,
    from_z,
    speeds,
    totals,
    coef,
    wet_cells,
    release,
    field,
    edge_out,
    edge_in,
    halo_send,
    halo_recv,
    x_send,
    x_recv,
    z_send,
    z_recv,
    speed_send,
    speed_recv,
    total_send,
    total_recv,
    edge_send,
    edge_recv,
):
    tags, rows, cols = tracer_ref.shape
    tile = depth_ref.shape[1]
    n_z = n_tag // 2
    place = lax.axis_index("tag")
    strip = lax.axis_index("strip")
    z, x = place // 2, place % 2
    other_x, other_strip = 1 - x, 1 - strip
    partner = z * 2 + other_x
    blocks = rows // 8

    def peer(k):
        result, bit = z, 1
        while bit < n_z:
            if k & bit:
                result = result + bit - 2 * bit * ((result // bit) % 2)
            bit *= 2
        return result

    def to(axis, index, src, dst, send, recv):
        return pltpu.make_async_remote_copy(
            src_ref=src,
            dst_ref=dst,
            send_sem=send,
            recv_sem=recv,
            device_id={axis: index},
            device_id_type=MESH,
        )

    def span(slot):
        return pl.ds(pl.multiple_of(slot * tile, tile), tile)

    sent = []

    def go(copy):
        copy.start()
        sent.append(copy)

    loads = [
        pltpu.make_async_copy(src, dst, load_sem.at[n])
        for n, (src, dst) in enumerate(
            (
                (depth_hbm, depth_ref),
                (bed_hbm, bed_ref),
                (east_hbm, east_ref),
                (south_hbm, south_ref),
                (tracer_hbm, tracer_ref),
                (code_hbm, code_ref),
                (wet_hbm, wet_ref),
                (outfall_hbm, outfall_ref),
                (loads_hbm, loads_ref),
            )
        )
    ]
    for load in loads:
        load.start()

    barrier = pltpu.get_barrier_semaphore()
    cols_in[...] = jnp.zeros_like(cols_in)
    for k in range(1, n_tag):
        pl.semaphore_signal(
            barrier, inc=1, device_id={"tag": lax.rem(place + k, n_tag)}, device_id_type=MESH
        )
    pl.semaphore_signal(barrier, inc=1, device_id={"strip": other_strip}, device_id_type=MESH)

    for load in loads[:4]:
        load.wait()
    water = depth_ref[...]
    east = east_ref[...]
    south = south_ref[...]
    surface = water + bed_ref[...]
    first = lax.broadcasted_iota(jnp.int32, (rows, 128), 1) == 0
    cols_out[0] = jnp.where(first, east[:, 0:1], surface[:, 0:1])
    cols_out[1] = jnp.where(first, east[:, tile - 1 : tile], surface[:, tile - 1 : tile])
    upper = strip == 0
    edge_first = lax.broadcasted_iota(jnp.int32, (8, tile), 0) == 0
    rows_out[...] = jnp.where(
        edge_first,
        jnp.where(upper, south[rows - 1 : rows], south[0:1]),
        jnp.where(upper, surface[rows - 1 : rows], surface[0:1]),
    )
    edge_out[...] = jnp.zeros_like(edge_out)
    loads[4].wait()
    for f in range(tags):
        edge_out[0, f : f + 1, :] = jnp.where(
            upper, tracer_ref[f, rows - 1 : rows, :], tracer_ref[f, 0:1, :]
        )
    for slot in range(n_tag):
        share = tracer_ref[0, :, slot * tile : (slot + 1) * tile]
        for f in range(1, tags):
            share = share + tracer_ref[f, :, slot * tile : (slot + 1) * tile]
        part[slot % 2, slot // 2] = share

    pl.semaphore_wait(barrier, n_tag)

    to_west = to("tag", place - 1, cols_out.at[0], cols_in.at[1], halo_send.at[0], halo_recv.at[1])
    to_east = to("tag", place + 1, cols_out.at[1], cols_in.at[0], halo_send.at[1], halo_recv.at[0])
    to_strip = to("strip", other_strip, rows_out, rows_in, halo_send.at[2], halo_recv.at[2])

    @pl.when(place > 0)
    def _():
        to_west.start()

    @pl.when(place < n_tag - 1)
    def _():
        to_east.start()

    go(to_strip)
    for k in reversed(range(n_z)):
        go(
            to(
                "tag",
                partner,
                part.at[other_x, peer(k)],
                from_x.at[k],
                x_send.at[k],
                x_recv.at[k],
            )
        )
    go(to("strip", other_strip, edge_out.at[0], edge_in.at[0], edge_send.at[0], edge_recv.at[0]))

    @pl.when(place > 0)
    def _():
        to_east.wait_recv()

    @pl.when(place < n_tag - 1)
    def _():
        to_west.wait_recv()

    to_strip.wait_recv()
    for load in loads[5:]:
        load.wait()
    lane = lax.broadcasted_iota(jnp.int32, (rows, tile), 1)
    row = lax.broadcasted_iota(jnp.int32, (rows, tile), 0)

    def west_of(cells, edge):
        return jnp.where(lane == 0, edge, pltpu.roll(cells, 1, 1))

    def east_of(cells, edge):
        return jnp.where(lane == tile - 1, edge, pltpu.roll(cells, tile - 1, 1))

    def north_of(cells, edge):
        return jnp.where(row == 0, jnp.where(upper, 0.0, edge), pltpu.roll(cells, 1, 0))

    def south_of(cells, edge):
        return jnp.where(row == rows - 1, jnp.where(upper, edge, 0.0), pltpu.roll(cells, rows - 1, 0))

    west_in, east_in, strip_in = cols_in[0], cols_in[1], rows_in[...]
    divergence = 0.5 * (
        east_of(east, east_in[:, 0:1]) - west_of(east, west_in[:, 0:1])
    ) + 0.5 * (south_of(south, strip_in[0:1]) - north_of(south, strip_in[0:1]))
    depth_next = water - STEP_RATIO * divergence
    own_codes = code_ref[:, span(place)]
    own_wet = wet_ref[:, span(place)].astype(jnp.float32)
    friction = 1.0 + pick(own_codes, FRICTION_TABLE)
    slope_east = 0.5 * (east_of(surface, east_in[:, 1:2]) - west_of(surface, west_in[:, 1:2]))
    slope_south = 0.5 * (south_of(surface, strip_in[1:2]) - north_of(surface, strip_in[1:2]))
    east_next = (east - GRAVITY_STEP * water * slope_east) / friction
    south_next = (south - GRAVITY_STEP * water * slope_south) / friction
    depth_out[...] = depth_next
    east_out[...] = east_next
    south_out[...] = south_next
    speeds[place, 0] = own_wet * east_next / depth_next
    speeds[place, 1] = own_wet * south_next / depth_next

    def gather(held, send, recv):
        for k in range(1, n_z):
            go(to("tag", peer(k) * 2 + x, held.at[place], held.at[place], send.at[k], recv.at[place]))
        go(to("tag", partner, held.at[place], held.at[place], send.at[0], recv.at[place]))

    def arrived(held, send, recv, slot):
        to("tag", partner, held.at[slot], held.at[slot], send.at[0], recv.at[slot]).wait_recv()

    def pass_on(held, send, recv, k):
        slot = peer(k) * 2 + x
        arrived(held, send, recv, slot)
        go(to("tag", partner, held.at[slot], held.at[slot], send.at[n_z - 1 + k], recv.at[slot]))

    gather(speeds, speed_send, speed_recv)

    for k in reversed(range(n_z)):
        into = from_x.at[k]
        to("tag", partner, into, into, x_send.at[k], x_recv.at[k]).wait_recv()
        red[k] = part[x, peer(k)] + into[...]
        if k:
            go(to("tag", peer(k) * 2 + x, red.at[k], from_z.at[k], z_send.at[k], z_recv.at[k]))

    def prepare(i, carry):
        at = pl.multiple_of(i * 8, 8)
        ids = (
            (strip * rows + at + lax.broadcasted_iota(jnp.int32, (8, cols), 0)) * COLUMNS
            + lax.broadcasted_iota(jnp.int32, (8, cols), 1)
        )
        for f in range(tags):
            t = place * tags + f
            release[f, pl.ds(at, 8), :] = jnp.where(
                ids == outfall_ref[t], SOURCE_STEP * loads_ref[t], 0.0
            )
            field[0, f, pl.ds(at + 8, 8), :] = tracer_ref[f, pl.ds(at, 8), :]
        all_tags = jnp.zeros((8, cols), jnp.float32)
        for t in range(outfall_ref.shape[0]):
            all_tags = all_tags + jnp.where(ids == outfall_ref[t], SOURCE_STEP * loads_ref[t], 0.0)
        release[tags, pl.ds(at, 8), :] = all_tags
        wet_cells[pl.ds(at, 8), :] = wet_ref[pl.ds(at, 8), :].astype(jnp.float32)
        return carry

    pass_on(speeds, speed_send, speed_recv, 1)
    lax.fori_loop(0, blocks, prepare, 0)
    for k in range(2, n_z):
        pass_on(speeds, speed_send, speed_recv, k)

    own_total = red[0]
    for k in range(1, n_z):
        to("tag", partner, red.at[k], from_z.at[k], z_send.at[k], z_recv.at[k]).wait_recv()
        own_total = own_total + from_z[k]
    totals[place] = own_total
    gather(totals, total_send, total_recv)

    def weigh(slot):
        go_east = speeds[slot, 0]
        go_south = speeds[slot, 1]
        spread = pick(code_ref[:, span(slot)], DISPERSION_TABLE)
        west = spread + COURANT * jnp.maximum(go_east, 0.0)
        east = spread - COURANT * jnp.minimum(go_east, 0.0)
        north = spread + COURANT * jnp.maximum(go_south, 0.0)
        south = spread - COURANT * jnp.minimum(go_south, 0.0)
        coef[0, :, span(slot)] = 1.0 - ((west + east) + (north + south))
        column = slot * tile + lane
        coef[1, :, span(slot)] = jnp.where(column == 0, 0.0, west)
        coef[2, :, span(slot)] = jnp.where(column == cols - 1, 0.0, east)
        coef[3, :, span(slot)] = jnp.where((row == 0) & upper, 0.0, north)
        coef[4, :, span(slot)] = jnp.where((row == rows - 1) & (strip == 1), 0.0, south)

    def settle(slot):
        field[0, tags, 8 : 8 + rows, span(slot)] = totals[slot]

    weigh(place)
    for k in range(1, n_z):
        weigh(peer(k) * 2 + x)
    for k in range(1, n_z):
        pass_on(totals, total_send, total_recv, k)
        settle(peer(k) * 2 + x)
    settle(place)
    for k in range(n_z):
        slot = peer(k) * 2 + other_x
        arrived(speeds, speed_send, speed_recv, slot)
        weigh(slot)
    for k in range(n_z):
        slot = peer(k) * 2 + other_x
        arrived(totals, total_send, total_recv, slot)
        settle(slot)

    last = jnp.where(upper, blocks - 1, 0)

    def edge_row(now, f):
        return jnp.where(
            upper, field[now, f, 7 + rows : 8 + rows, :], field[now, f, 8:9, :]
        )

    def exchange(n):
        return to(
            "strip", other_strip, edge_out.at[n], edge_in.at[n], edge_send.at[n], edge_recv.at[n]
        )

    edge_out[1, tags : tags + 1, :] = edge_row(0, tags)
    go(exchange(1))

    def put_halo(n, now, fields):
        for f in fields:
            got = edge_in[n, f : f + 1, :]
            field[now, f, 7:8, :] = got
            field[now, f, 8 + rows : 9 + rows, :] = got

    exchange(0).wait_recv()
    put_halo(0, 0, range(tags))
    exchange(1).wait_recv()
    put_halo(1, 0, [tags])

    for substep in range(SUBSTEPS):
        now, later = substep % 2, 1 - substep % 2
        ends = substep == SUBSTEPS - 1
        if substep:
            exchange(substep + 1).wait_recv()
            put_halo(substep + 1, now, range(tags + 1))

        def block(i, carry):
            at = pl.multiple_of(lax.rem(last + i, blocks) * 8, 8)
            here = pl.ds(at, 8)
            rate = wet_cells[here, :] / (1.0 + DECAY_RATE * field[now, tags, pl.ds(at + 8, 8), :])
            for f in range(tags if ends else tags + 1):
                wide = field[now, f, pl.ds(at, 24), :]
                cell = wide[8:16]
                value = (
                    coef[0, here, :] * cell
                    + coef[1, here, :] * pltpu.roll(cell, 1, 1)
                    + coef[2, here, :] * pltpu.roll(cell, cols - 1, 1)
                    + coef[3, here, :] * wide[7:15]
                    + coef[4, here, :] * wide[9:17]
                    + release[f, here, :]
                ) * rate
                if ends:
                    tracer_out[f, here, :] = value
                else:
                    field[later, f, pl.ds(at + 8, 8), :] = value
            if not ends:

                @pl.when(i == 0)
                def _():
                    for f in range(tags + 1):
                        edge_out[substep + 2, f : f + 1, :] = edge_row(later, f)
                    exchange(substep + 2).start()

            return carry

        lax.fori_loop(0, blocks, block, 0)

    for n in range(SUBSTEPS - 1):
        exchange(n + 2).wait_send()
    for copy in sent:
        copy.wait_send()

    @pl.when(place > 0)
    def _():
        to_west.wait_send()

    @pl.when(place < n_tag - 1)
    def _():
        to_east.wait_send()


def store_kernel(*refs):
    sem = refs[8]
    copies = [pltpu.make_async_copy(refs[n], refs[4 + n], sem.at[n]) for n in range(4)]
    for copy in copies:
        copy.start()
    for copy in copies:
        copy.wait()


def fused(n_tag, *arrays):
    tracer, water = arrays[0], arrays[1]
    tags, rows, cols = tracer.shape
    tile = water.shape[1]
    n_z = n_tag // 2
    f32 = jnp.float32
    dma = pltpu.SemaphoreType.DMA
    vmem = pl.BlockSpec(memory_space=pltpu.VMEM)
    hbm = pl.BlockSpec(memory_space=pltpu.HBM)
    plane = jax.ShapeDtypeStruct(water.shape, f32)
    results = pl.pallas_call(
        functools.partial(flood_kernel, n_tag),
        out_shape=(jax.ShapeDtypeStruct(tracer.shape, f32), plane, plane, plane),
        in_specs=[hbm] * 9,
        out_specs=(vmem,) * 4,
        scratch_shapes=[
            *[pltpu.VMEM(a.shape, a.dtype) for a in arrays[:7]],
            *[pltpu.SMEM(a.shape, a.dtype) for a in arrays[7:]],
            dma((9,)),
            pltpu.VMEM((2, rows, 128), f32),
            pltpu.VMEM((2, rows, 128), f32),
            pltpu.VMEM((8, tile), f32),
            pltpu.VMEM((8, tile), f32),
            pltpu.VMEM((2, n_z, rows, tile), f32),
            pltpu.VMEM((n_z, rows, tile), f32),
            pltpu.VMEM((n_z, rows, tile), f32),
            pltpu.VMEM((n_z, rows, tile), f32),
            pltpu.VMEM((n_tag, 2, rows, tile), f32),
            pltpu.VMEM((n_tag, rows, tile), f32),
            pltpu.VMEM((5, rows, cols), f32),
            pltpu.VMEM((rows, cols), f32),
            pltpu.VMEM((tags + 1, rows, cols), f32),
            pltpu.VMEM((2, tags + 1, rows + 16, cols), f32),
            pltpu.VMEM((SUBSTEPS + 1, 8, cols), f32),
            pltpu.VMEM((SUBSTEPS + 1, 8, cols), f32),
            dma((3,)),
            dma((3,)),
            dma((n_z,)),
            dma((n_z,)),
            dma((n_z,)),
            dma((n_z,)),
            dma((2 * n_z - 1,)),
            dma((n_tag,)),
            dma((2 * n_z - 1,)),
            dma((n_tag,)),
            dma((SUBSTEPS + 1,)),
            dma((SUBSTEPS + 1,)),
        ],
        compiler_params=pltpu.CompilerParams(
            collective_id=0, has_side_effects=True, vmem_limit_bytes=60 * 1024 * 1024
        ),
    )(*arrays)
    return pl.pallas_call(
        store_kernel,
        out_shape=tuple(jax.ShapeDtypeStruct(r.shape, r.dtype) for r in results),
        in_specs=[vmem] * 4,
        out_specs=(hbm,) * 4,
        scratch_shapes=[dma((4,))],
        compiler_params=pltpu.CompilerParams(vmem_limit_bytes=60 * 1024 * 1024),
    )(*results)


def fits(n_tag, n_strip, tags, rows, cols):
    tile = cols // n_tag
    z_power = n_tag % 2 == 0 and (n_tag // 2) & (n_tag // 2 - 1) == 0
    return (
        n_strip == 2 and z_power and n_tag <= 16 and tile % 128 == 0 and rows % 8 == 0 and tags < 8
    )


def solution(mesh):
    in_specs = (
        P(("runs", "tag"), "strip", None),
        P(("runs", "strip"), "tag"),
        P(("runs", "strip"), "tag"),
        P(("runs", "strip"), "tag"),
        P("strip", "tag"),
        P(("runs", "strip"), None),
        P("strip", None),
        P(),
        P("runs"),
    )
    out_specs = (
        P(("runs", "tag"), "strip", None),
        P(("runs", "strip"), "tag"),
        P(("runs", "strip"), "tag"),
        P(("runs", "strip"), "tag"),
    )

    def local(*arrays):
        n_tag, n_strip = mesh.shape["tag"], mesh.shape["strip"]
        if fits(n_tag, n_strip, *arrays[0].shape):
            return fused(n_tag, *arrays)
        return shards(*arrays)

    return jax.shard_map(local, mesh=mesh, in_specs=in_specs, out_specs=out_specs, check_vma=False)
```
